128 devices in a mesh: rows: 32 (over x, y, z_hi), cols: 4 (over z_lo, core).
Axes of the slice: x: 4, y: 4, z: 4 (z_hi: 2, z_lo: 2; z = z_hi * 2 + z_lo), core: 2. Of those that a mesh axis runs over, the one named last changes fastest.
Arguments:
- counts: int32 [8192, 65536], P('rows', 'cols'), may hold values from 0 to 11
- row_marg: int32 [8192], P('rows'), may hold values from 16384 to 131071
- ctx_marg: int32 [65536], P('cols'), may hold values from 1 to 113554
- discount: int32 [65536], P('cols'), may hold values from 1 to 5
- probes: bfloat16 [65536, 256], P('cols'), may hold values from -0.0234375 to 0.0234375
Outputs:
- y_proj: bfloat16 [8192, 256], P('rows')
- z_proj: float32 [4, 16384, 256], P('cols', 'rows')
The draws below stay inside these ranges and needn't reach their ends.
All inputs are finite; a program needn't handle non-finite values.
Results may differ from the reference program's by a relative error of at most 0.005.
Values may be sent and summed in bfloat16 or wider, within the bound.
No kernel may reach another device: no remote copies, remote signals or barrier semaphores. Data moves between devices by JAX's collectives and lax.ppermute only.
A program may use at most 128 MiB of HBM per device.

```python
import jax
import jax.numpy as jnp
from jax import lax

ROWS_DEV = 256
CONTEXTS = 65536
PROBES = 256
ROWS = 8192
N_COLS = 4


def draw_counts(key, part):
    key = jax.random.fold_in(key, 11)
    perm_key, keep_key, value_key = jax.random.split(key, 3)
    order = jax.random.permutation(perm_key, CONTEXTS).astype(jnp.int32)
    group_of = order * 256 // CONTEXTS
    kept = jax.random.randint(keep_key, (ROWS, 256), 0, 2).astype(jnp.int32)
    row_mask = jnp.take(kept, group_of, axis=1)
    values = jax.random.randint(value_key, (ROWS, CONTEXTS), 0, 12).astype(jnp.int32)
    return (values * row_mask).astype(jnp.int32)


def draw_ctx_marg(key, part):
    key = jax.random.fold_in(key, 7)
    first_key, second_key = jax.random.split(key)
    factor_a = jax.random.randint(first_key, (CONTEXTS,), 0, 1024)
    quarter = jnp.arange(CONTEXTS, dtype=jnp.int32) * 4 // CONTEXTS
    upper = 16 * (1 + 2 * quarter)
    factor_b = jax.random.randint(second_key, (CONTEXTS,), 0, 1 << 20) % upper
    return (1 + factor_a * factor_b).astype(jnp.int32)


def set_ends(array, key, smallest, high):
    extent = array.shape
    index_at = [jax.random.randint(jax.random.fold_in(key, axis), (), 0, extent[axis]) for axis in range(len(extent))]
    array = array.at[tuple(index_at)].set(smallest)
    longest = extent.index(max(extent))
    index_at[longest] = (index_at[longest] + 1) % extent[longest]
    return array.at[tuple(index_at)].set(high)


def levels(stream_key, dims, pieces, least, high):
    def one(position, parts):
        steps = jax.random.uniform(jax.random.fold_in(jax.random.fold_in(stream_key, 6), position), (parts,), jnp.float32, least / len(pieces), high / len(pieces))
        return jnp.repeat(jnp.exp(steps), dims[position] // parts).reshape((-1,) + (1,) * (len(dims) - position - 1))

    factor_of = one(*pieces[0])
    for cut in pieces[1:]:
        factor_of = factor_of * one(*cut)
    return factor_of


def normal_values(stream_key, extent, deviation, bound, cuts=(), kind=jnp.bfloat16):
    result = jax.random.normal(stream_key, extent, jnp.float32) * deviation
    if len(cuts) > 0:
        result = levels(stream_key, extent, cuts, -0.22, 0.18) * result
    return jnp.clip(result, min=-bound, max=bound).astype(kind)


def setup_inputs(seed: int = 0) -> dict:
    splits = jax.random.split(jax.random.key(seed), 6)
    counts = draw_counts(jax.random.fold_in(splits[5], 71), 0)
    row_marg = set_ends(jax.random.randint(splits[1], (ROWS,), CONTEXTS // 4, CONTEXTS * 2), jax.random.fold_in(splits[1], 1), CONTEXTS // 4, (CONTEXTS * 2) - 1).astype(jnp.int32)
    ctx_marg = draw_ctx_marg(jax.random.fold_in(splits[5], 71), 0)
    discount = set_ends(jax.random.randint(splits[3], (CONTEXTS,), 1, 6), jax.random.fold_in(splits[3], 1), 1, 5).astype(jnp.int32)
    probes = normal_values(splits[4], (CONTEXTS, PROBES), CONTEXTS ** -0.5, 0.0234375, ((0, 4),))
    return {"counts": counts, "row_marg": row_marg, "ctx_marg": ctx_marg, "discount": discount, "probes": probes}


def ppmi_tile(counts, log_row, ctx_term, log_total, shrink):
    excess = counts.astype(jnp.float32) - shrink[None, :]
    raw_pmi = jnp.log(jnp.maximum(excess, 0.25)) + log_total - log_row[:, None] - ctx_term[None, :]
    return jnp.where(excess > 0.0, jnp.maximum(raw_pmi, 0.0), 0.0).astype(jnp.bfloat16)


def reference(counts, row_marg, ctx_marg, discount, probes):
    shrink = discount.astype(jnp.float32) * 0.25
    log_ctx = jnp.log(ctx_marg.astype(jnp.float32))
    ctx_term = 0.75 * log_ctx
    log_total = jnp.log(jnp.sum(jnp.exp(ctx_term)))
    log_row = jnp.log(row_marg.astype(jnp.float32))
    steps_n = ROWS // ROWS_DEV
    count_blocks = counts.reshape(steps_n, ROWS_DEV, CONTEXTS)
    row_blocks = log_row.reshape(steps_n, ROWS_DEV)

    def advance(summed, pair):
        block_counts, block_row = pair
        tile = ppmi_tile(block_counts, block_row, ctx_term, log_total, shrink)
        y_block = jnp.dot(tile, probes, preferred_element_type=jnp.float32).astype(jnp.bfloat16)
        part = lax.dot_general(tile, y_block, (((0,), (0,)), ((), ())), preferred_element_type=jnp.float32)
        summed = summed + part
        return summed, y_block

    summed, y_blocks = lax.scan(advance, jnp.zeros((CONTEXTS, PROBES), jnp.float32), (count_blocks, row_blocks))
    y_proj = y_blocks.reshape(ROWS, PROBES)
    z_proj = (summed * ROWS ** -0.5).reshape(N_COLS, CONTEXTS // N_COLS, PROBES)
    return y_proj, z_proj
```

```python
import functools

import jax
import jax.numpy as jnp
import numpy as np
from jax import lax
from jax.experimental import pallas as pl
from jax.experimental.pallas import tpu as pltpu

from jax.sharding import PartitionSpec as P

AXES = ("rows", "cols")
W = 256
PACK = 8
F32, BF16 = jnp.float32, jnp.bfloat16


def device_id(x, y, zh, zl, core):
    return (x * 8 + y * 2 + zh) * 4 + zl * 2 + core


def flip(kind, a):
    return a ^ 1 if kind == 0 else 3 - a


def all_devices():
    for x in range(4):
        for y in range(4):
            for zh in range(2):
                for zl in range(2):
                    for core in range(2):
                        yield x, y, zh, zl, core


def ring_perm(kind, second_axis):
    pairs = []
    for x, y, zh, zl, core in all_devices():
        if (core == 0) != second_axis:
            to = device_id(flip(kind, x), y, zh, zl, core)
        else:
            to = device_id(x, flip(kind, y), zh, zl, core)
        pairs.append((device_id(x, y, zh, zl, core), to))
    return pairs


ZH_PERM = [(device_id(*d), device_id(d[0], d[1], 1 - d[2], d[3], d[4])) for d in all_devices()]
ZL_PERM = [(device_id(*d), device_id(d[0], d[1], d[2], 1 - d[3], d[4])) for d in all_devices()]
CORE_PERM = [(device_id(*d), device_id(d[0], d[1], d[2], d[3], 1 - d[4])) for d in all_devices()]


def block_order():
    table = np.zeros((128, 4, 16), np.int32)
    for d in all_devices():
        x, y, zh, zl, core = d
        u, v = (x, y) if core == 0 else (y, x)
        for g in range(2):
            near, far = g, 1 - g
            vs = [v, flip(far, v), flip(near, v), flip(far, flip(near, v))]
            for part, start in enumerate((u, flip(near, u))):
                us = [start, flip(far, start)]
                blocks = []
                for i in us:
                    for j in vs:
                        for k in (zh, 1 - zh):
                            own = (i * 8 + j * 2 + k) if core == 0 else (j * 8 + i * 2 + k)
                            blocks.append(own * 2 + g)
                table[device_id(*d), 2 * g + part] = blocks
    return table.reshape(128, 64)


ORDER = block_order()


def permute(a, perm):
    return lax.ppermute(a, AXES, perm)


def params(mib):
    return pltpu.CompilerParams(vmem_limit_bytes=mib << 20)


def context_kernel(marg_ref, disc_ref, power_ref, shrink_ref, total_ref):
    power = jnp.exp(0.75 * jnp.log(marg_ref[...].astype(F32)))
    power_ref[...] = 1.0 / power
    shrink_ref[...] = disc_ref[...].astype(F32) * 0.25
    total_ref[...] = jnp.full((8, 128), jnp.sum(power), F32)


def context(ctx_marg, discount):
    shape = jax.ShapeDtypeStruct((64, W), F32)
    return pl.pallas_call(
        context_kernel,
        out_shape=(shape, shape, jax.ShapeDtypeStruct((8, 128), F32)),
        cost_estimate=pl.CostEstimate(flops=1 << 16, bytes_accessed=1 << 18, transcendentals=1 << 15),
    )(ctx_marg.reshape(64, W), discount.reshape(64, W))


def send_kernel(order_ref, *refs):
    for k in range(PACK):
        refs[PACK][k] = refs[k][...].astype(F32).astype(BF16)


def counts_to_send(order, counts, first):
    rows = counts.shape[0]
    specs = [
        pl.BlockSpec((rows, W), functools.partial(lambda k, i, o: (0, o[first + i * PACK + k]), k))
        for k in range(PACK)
    ]
    return pl.pallas_call(
        send_kernel,
        grid_spec=pltpu.PrefetchScalarGridSpec(
            num_scalar_prefetch=1,
            grid=(16 // PACK,),
            in_specs=specs,
            out_specs=pl.BlockSpec((PACK, rows, W), lambda i, o: (i, 0, 0)),
        ),
        out_shape=jax.ShapeDtypeStruct((16, rows, W), BF16),
        compiler_params=params(40),
        cost_estimate=pl.CostEstimate(flops=1 << 20, bytes_accessed=6 << 20, transcendentals=0),
    )(order, *([counts] * PACK))


def tile_rows(counts, shrink, scale, inv_row):
    excess = counts.astype(F32) - shrink
    return jnp.log(jnp.maximum(excess * scale * inv_row, 1.0)).astype(BF16)


def forward_kernel(order_ref, total_ref, row_ref, power_ref, shrink_ref, *refs):
    counts, probes = refs[:PACK], refs[PACK:2 * PACK]
    tile_ref, y_ref, acc_ref, work_ref = refs[2 * PACK:]
    step = pl.program_id(0)

    @pl.when(step == 0)
    def _():
        acc_ref[...] = jnp.zeros_like(acc_ref)

    total = total_ref[0, 0]
    rows = row_ref.shape[0]
    part = None
    for k in range(PACK):
        block = order_ref[step * PACK + k]
        shrink = shrink_ref[pl.ds(block, 1), :]
        scale = power_ref[pl.ds(block, 1), :] * total
        for r in range(0, rows, 32):
            inv_row = row_ref[r:r + 32, :]
            work_ref[k, r:r + 32, :] = tile_rows(counts[k][r:r + 32, :], shrink, scale, inv_row)
        term = jnp.dot(work_ref[k], probes[k][...], preferred_element_type=F32)
        part = term if part is None else part + term
    acc_ref[...] += part

    @pl.when((step & 3) < 2)
    def _():
        tile_ref[...] = work_ref[...]

    @pl.when(step == pl.num_programs(0) - 1)
    def _():
        y_ref[...] = jnp.transpose(acc_ref[...])


def forward(order, total, inv_row, power, shrink, counts, probes):
    rows, width = counts.shape[0], probes.shape[1]
    steps = 64 // PACK
    count_specs = [
        pl.BlockSpec((rows, W), functools.partial(lambda k, i, o: (0, o[i * PACK + k]), k)) for k in range(PACK)
    ]
    probe_specs = [
        pl.BlockSpec((W, width), functools.partial(lambda k, i, o: (o[i * PACK + k], 0), k)) for k in range(PACK)
    ]
    whole = lambda shape: pl.BlockSpec(shape, lambda i, o: (0, 0))
    return pl.pallas_call(
        forward_kernel,
        grid_spec=pltpu.PrefetchScalarGridSpec(
            num_scalar_prefetch=1,
            grid=(steps,),
            in_specs=[
                pl.BlockSpec(memory_space=pltpu.SMEM),
                whole((rows, 1)),
                whole((64, W)),
                whole((64, W)),
                *count_specs,
                *probe_specs,
            ],
            out_specs=[
                pl.BlockSpec((PACK, rows, W), lambda i, o: (2 * (i // 4) + jnp.minimum(i % 4, 1), 0, 0)),
                whole((width, rows)),
            ],
            scratch_shapes=[pltpu.VMEM((rows, width), F32), pltpu.VMEM((PACK, rows, W), BF16)],
        ),
        out_shape=(
            jax.ShapeDtypeStruct((32, rows, W), BF16),
            jax.ShapeDtypeStruct((width, rows), F32),
        ),
        compiler_params=params(48),
        cost_estimate=pl.CostEstimate(flops=1 << 31, bytes_accessed=28 << 20, transcendentals=1 << 22),
    )(order, total, inv_row, power, shrink, *([counts] * PACK), *([probes] * PACK))


def back_kernel(base, order_ref, total_ref, row_ref, power_ref, shrink_ref, y_own_ref, y_other_ref, tile_ref, count_ref, z_ref, work_ref):
    step = pl.program_id(0)
    total = total_ref[0, 0]
    n, rows, _ = tile_ref.shape
    for k in range(n):
        block = order_ref[base + step * n + k]
        shrink = shrink_ref[pl.ds(block, 1), :]
        scale = power_ref[pl.ds(block, 1), :] * total
        for r in range(0, rows, 32):
            inv_row = row_ref[r:r + 32, :]
            work_ref[k, r:r + 32, :] = tile_rows(count_ref[k, r:r + 32, :], shrink, scale, inv_row)
        out = jnp.dot(y_own_ref[...], tile_ref[k], preferred_element_type=F32)
        out = out + jnp.dot(y_other_ref[...], work_ref[k], preferred_element_type=F32)
        z_ref[k] = out.astype(z_ref.dtype)


def back(order, total, inv_row, power, shrink, y_own, y_other, tile, received, group, half, dtype):
    n = 4
    rows, width = tile.shape[1], y_own.shape[0]
    tile_at = (group * 16 + half * 8) // n
    count_at = half * 8 // n
    whole = lambda shape: pl.BlockSpec(shape, lambda i, o: (0, 0))
    return pl.pallas_call(
        functools.partial(back_kernel, group * 32 + half * 8),
        grid_spec=pltpu.PrefetchScalarGridSpec(
            num_scalar_prefetch=1,
            grid=(8 // n,),
            in_specs=[
                pl.BlockSpec(memory_space=pltpu.SMEM),
                whole((rows, 1)),
                whole((64, W)),
                whole((64, W)),
                whole((width, rows)),
                whole((width, rows)),
                pl.BlockSpec((n, rows, W), lambda i, o: (tile_at + i, 0, 0)),
                pl.BlockSpec((n, rows, W), lambda i, o: (count_at + i, 0, 0)),
            ],
            out_specs=pl.BlockSpec((n, width, W), lambda i, o: (i, 0, 0)),
            scratch_shapes=[pltpu.VMEM((n, rows, W), BF16)],
        ),
        out_shape=jax.ShapeDtypeStruct((8, width, W), dtype),
        compiler_params=params(32),
        cost_estimate=pl.CostEstimate(flops=1 << 29, bytes_accessed=4 << 20, transcendentals=1 << 19),
    )(order, total, inv_row, power, shrink, y_own, y_other, tile, received)


def local(counts, row_marg, ctx_marg, discount, probes):
    me = lax.axis_index("rows") * 4 + lax.axis_index("cols")
    order = lax.dynamic_index_in_dim(jnp.asarray(ORDER), me, 0, keepdims=False)
    first = [ring_perm(g, False) for g in range(2)]
    second = [ring_perm(1 - g, False) for g in range(2)]
    third = [ring_perm(g, True) for g in range(2)]
    fourth = [ring_perm(1 - g, True) for g in range(2)]

    power, shrink, total = context(ctx_marg, discount)
    total = total + permute(total, CORE_PERM)
    total = total + permute(total, ZL_PERM)
    inv_row = (1.0 / row_marg.astype(F32))[:, None]

    received = [permute(counts_to_send(order, counts, 32 * g + 16), first[g]) for g in range(2)]
    inv_other = [permute(inv_row, first[g]) for g in range(2)]

    tile, y_part = forward(order, total, inv_row, power, shrink, counts, probes)
    y_part = y_part + permute(y_part, CORE_PERM)
    y_part = y_part + permute(y_part, ZL_PERM)
    y_own = y_part.astype(BF16)
    y_other = [permute(y_own, first[g]) for g in range(2)]

    def run(g, half, dtype):
        return back(order, total, inv_other[g], power, shrink, y_own, y_other[g], tile, received[g], g, half, dtype)

    out = []
    sends = [run(g, 1, BF16) for g in range(2)]
    for g in range(2):
        r2 = permute(sends[g], second[g]).astype(F32)
        z = run(g, 0, F32)
        r3 = permute((z[4:8] + r2[4:8]).astype(BF16), third[g]).astype(F32)
        r4 = permute((z[2:4] + r2[2:4] + r3[2:4]).astype(BF16), fourth[g]).astype(F32)
        r5 = permute((z[1] + r2[1] + r3[1] + r4[1]).astype(BF16), ZH_PERM).astype(F32)
        out.append(jnp.transpose(z[0] + r2[0] + r3[0] + r4[0] + r5))
    row_devices = lax.axis_size("rows")
    factor = (counts.shape[0] * row_devices) ** (-0.5)
    z_proj = jnp.concatenate(out, axis=0) * factor
    return (jnp.transpose(y_own), z_proj[None])


def solution(mesh):
    in_specs = (P("rows", "cols"), P("rows"), P("cols"), P("cols"), P("cols", None))
    out_specs = (P("rows", None), P("cols", "rows", None))
    return jax.shard_map(local, mesh=mesh, in_specs=in_specs, out_specs=out_specs, check_vma=False)
```

```python
import functools

import jax
import jax.numpy as jnp
from jax import lax
from jax.experimental import pallas as pl
from jax.experimental.pallas import tpu as pltpu
from jax.sharding import PartitionSpec as P

AXES = ("rows", "cols")
W = 256
STEP = 8
F32, BF16 = jnp.float32, jnp.bfloat16

NEAR, FAR = (1, 3), (3, 1)


def xor_perm(mask):
    pairs = []
    for d in range(128):
        r, zl, core = d >> 2, (d >> 1) & 1, d & 1
        dr, dzl, dcore = mask(core)
        pairs.append((d, ((r ^ dr) << 2) | ((zl ^ dzl) << 1) | (core ^ dcore)))
    return pairs


def u_perm(d):
    return xor_perm(lambda core: (d * (2 if core else 8), 0, 0))


def v_perm(d):
    return xor_perm(lambda core: (d * (8 if core else 2), 0, 0))


ZH_PERM = xor_perm(lambda core: (1, 0, 0))
ZL_PERM = xor_perm(lambda core: (0, 1, 0))
CORE_PERM = xor_perm(lambda core: (0, 0, 1))


def permute(a, perm):
    return lax.ppermute(a, AXES, perm)


def place():
    core = lax.rem(lax.axis_index("cols"), 2)
    return lax.axis_index("rows"), core


def block_of(r, core, g, d, e, k):
    return (r ^ (d * (8 - 6 * core) + e * (2 + 6 * core) + k)) * 2 + g


def slots(g, part):
    out = []
    for i in range(2):
        for j in range(4):
            for k in range(2):
                out.append(((NEAR[g] if part else 0) ^ (FAR[g] * i), (FAR[g] * (j & 1)) ^ (NEAR[g] * (j >> 1)), k))
    return out


def params(mib):
    return pltpu.CompilerParams(vmem_limit_bytes=mib << 20)


def spec(space):
    return pl.BlockSpec(memory_space=space)


def context_kernel(all_ref, power_ref, shrink_ref, total_ref, inv_ref, tail_ref):
    power = jnp.exp(0.75 * jnp.log(all_ref[0:128, :].astype(F32)))
    power_ref[...] = 1.0 / power
    shrink_ref[...] = all_ref[128:256, :].astype(F32) * 0.25
    total_ref[...] = jnp.full((8, 128), jnp.sum(power), F32)
    wide = jnp.concatenate([all_ref[256:257, :], all_ref[257:258, :]], axis=1)
    inv_ref[...] = 1.0 / jnp.transpose(jnp.broadcast_to(wide.astype(F32), (128, W)))
    at = lax.broadcasted_iota(jnp.int32, (16, W), 0)
    low, mid, high = wide & 63, (wide >> 6) & 63, wide >> 12
    tail_ref[...] = jnp.where(at == 0, low, jnp.where(at == 1, mid, high)).astype(F32).astype(BF16)


def context(ctx_marg, discount, row_marg):
    square = jax.ShapeDtypeStruct((128, 128), F32)
    return pl.pallas_call(
        context_kernel,
        in_specs=[spec(pltpu.VMEM)],
        out_specs=[spec(pltpu.VMEM)] * 5,
        out_shape=(square, square, jax.ShapeDtypeStruct((8, 128), F32), jax.ShapeDtypeStruct((W, 128), F32),
                   jax.ShapeDtypeStruct((16, W), BF16)),
        compiler_params=params(2),
        cost_estimate=pl.CostEstimate(flops=1 << 18, bytes_accessed=1 << 18, transcendentals=1 << 15),
    )(jnp.concatenate([ctx_marg, discount, row_marg]).reshape(258, 128))


def prepare_kernel(part, *refs):
    if part == 1:
        tail_ref, counts_ref, *outs, in_ref, sem = refs
        for out_ref in outs:
            out_ref[16 * W:16 * W + 16, :] = tail_ref[...]
    else:
        counts_ref, kept_ref, in_ref, sem = refs
    r, core = place()

    def fetch(s):
        d, e, k = slots(s // 16, part)[s % 16]
        at = pl.multiple_of(block_of(r, core, s // 16, d, e, k) * W, W)
        return pltpu.make_async_copy(counts_ref.at[:, pl.ds(at, W)], in_ref.at[s], sem.at[s])

    for s in range(32):
        fetch(s).start()
    for s in range(32):
        fetch(s).wait()
        block = in_ref[s].astype(F32).astype(BF16)
        if part == 1:
            outs[s // 16][s % 16 * W:(s % 16 + 1) * W, :] = block
        else:
            kept_ref[s * W:(s + 1) * W, :] = block


def prepare(part, counts, *tail):
    rows = counts.shape[0]
    lengths = [16 * W + 16] * 2 if part else [32 * W]
    return pl.pallas_call(
        functools.partial(prepare_kernel, part),
        in_specs=[spec(pltpu.VMEM)] * part + [spec(pl.ANY)],
        out_specs=[spec(pltpu.VMEM)] * len(lengths),
        out_shape=[jax.ShapeDtypeStruct((n, W), BF16) for n in lengths],
        scratch_shapes=[pltpu.VMEM((32, rows, W), jnp.int32), pltpu.SemaphoreType.DMA((32,))],
        compiler_params=params(42),
        cost_estimate=pl.CostEstimate(flops=1 << 22, bytes_accessed=12 << 20, transcendentals=0),
    )(*tail, counts)


def tile_rows(counts, shrink, scale, inv_row):
    inv_row = jnp.concatenate([inv_row, inv_row], axis=1)
    excess = counts.astype(F32) - shrink
    return jnp.log(jnp.maximum(excess * scale * inv_row, 1.0)).astype(BF16)


def column_terms(ref, block):
    return jnp.concatenate([ref[pl.ds(2 * block, 1), :], ref[pl.ds(2 * block + 1, 1), :]], axis=1)


def forward_kernel(total_ref, other_ref, inv_ref, power_ref, shrink_ref, kept_ref, sent_a, sent_b, probes_ref,
                   tile_ref, y_ref, acc_ref, work_ref):
    r, core = place()
    total = total_ref[0, 0] + other_ref[0, 0]
    rows = inv_ref.shape[0]
    acc_ref[...] = jnp.zeros_like(acc_ref)
    for g, sent_ref in enumerate((sent_a, sent_b)):
        for part in range(2):
            @pl.loop(0, 2)
            def _(i):
                sums = None
                for n, (d, e, k) in enumerate(slots(g, part)[:8]):
                    block = block_of(r, core, g, d ^ (FAR[g] * i), e, k)
                    at = pl.multiple_of(block * W, W)
                    shrink = column_terms(shrink_ref, block)
                    scale = column_terms(power_ref, block) * total
                    if part == 0:
                        source, base, out = kept_ref, (16 * g + 8 * i + n) * rows, tile_ref.at[16 * g + 8 * i + n]
                    else:
                        source, base, out = sent_ref, (8 * i + n) * rows, work_ref.at[n]
                    base = pl.multiple_of(base, rows)
                    for q in range(0, rows, 32):
                        out[q:q + 32, :] = tile_rows(source[pl.ds(base + q, 32), :], shrink, scale, inv_ref[q:q + 32, :])
                    term = jnp.dot(out[...], probes_ref[pl.ds(at, W), :], preferred_element_type=F32)
                    sums = term if sums is None else sums + term
                acc_ref[...] += sums
    y_ref[...] = jnp.transpose(acc_ref[...])


def forward(total, other, inv_row, power, shrink, kept, sent, probes):
    rows, width = inv_row.shape[0], probes.shape[1]
    vmem, smem = spec(pltpu.VMEM), spec(pltpu.SMEM)
    return pl.pallas_call(
        forward_kernel,
        in_specs=[smem, smem] + [vmem] * 7,
        out_specs=[vmem, vmem],
        scratch_shapes=[pltpu.VMEM((rows, width), F32), pltpu.VMEM((STEP, rows, W), BF16)],
        out_shape=(jax.ShapeDtypeStruct((32, rows, W), BF16), jax.ShapeDtypeStruct((width, rows), F32)),
        compiler_params=params(4),
        cost_estimate=pl.CostEstimate(flops=1 << 31, bytes_accessed=28 << 20, transcendentals=1 << 22),
    )(total, other, inv_row, power, shrink, kept, *sent, probes)


def back_kernel(group, half, total_ref, other_ref, power_ref, shrink_ref, y_own_ref, y_other_ref, tile_ref, count_ref,
                z_ref, work_ref, inv_ref):
    r, core = place()
    total = total_ref[0, 0] + other_ref[0, 0]
    rows = tile_ref.shape[1]
    tail = count_ref[16 * W:16 * W + 16, :].astype(F32)
    marg = tail[0:1, :] + tail[1:2, :] * 64.0 + tail[2:3, :] * 4096.0
    inv_ref[...] = 1.0 / jnp.transpose(jnp.broadcast_to(marg, (128, rows)))
    for n in range(8):
        s = half * 8 + n
        d, e, k = slots(group, 0)[s]
        block = block_of(r, core, group, d, e, k)
        shrink = column_terms(shrink_ref, block)
        scale = column_terms(power_ref, block) * total
        for i in range(0, rows, 32):
            work_ref[n, i:i + 32, :] = tile_rows(
                count_ref[s * W + i:s * W + i + 32, :], shrink, scale, inv_ref[i:i + 32, :])
        out = jnp.dot(y_own_ref[...], tile_ref[group * 16 + s], preferred_element_type=F32)
        out = out + jnp.dot(y_other_ref[...], work_ref[n], preferred_element_type=F32)
        z_ref[n] = out.astype(z_ref.dtype)


def back(total, other, power, shrink, y_own, y_other, tile, received, group, half, dtype):
    rows, width = tile.shape[1], y_own.shape[0]
    vmem, smem = spec(pltpu.VMEM), spec(pltpu.SMEM)
    return pl.pallas_call(
        functools.partial(back_kernel, group, half),
        in_specs=[smem, smem] + [vmem] * 6,
        out_specs=vmem,
        scratch_shapes=[pltpu.VMEM((8, rows, W), BF16), pltpu.VMEM((rows, 128), F32)],
        out_shape=jax.ShapeDtypeStruct((8, width, W), dtype),
        compiler_params=params(4),
        cost_estimate=pl.CostEstimate(flops=1 << 29, bytes_accessed=4 << 20, transcendentals=1 << 19),
    )(total, other, power, shrink, y_own, y_other, tile, received)


def pair_kernel(a_ref, b_ref, out_ref):
    out_ref[0] = a_ref[...]
    out_ref[1] = b_ref[...]


def pair(a, b):
    vmem = spec(pltpu.VMEM)
    return pl.pallas_call(
        pair_kernel,
        in_specs=[vmem, vmem],
        out_specs=vmem,
        out_shape=jax.ShapeDtypeStruct((2,) + a.shape, a.dtype),
        compiler_params=params(1),
        cost_estimate=pl.CostEstimate(flops=0, bytes_accessed=1 << 19, transcendentals=0),
    )(a, b)


def last_kernel(factor, a_ref, b_ref, got_ref, z_ref):
    for g, ref in enumerate((a_ref, b_ref)):
        z_ref[g * W:(g + 1) * W, :] = jnp.transpose(ref[...] + got_ref[g].astype(F32)) * factor


def last(a, b, got, factor):
    width = a.shape[0]
    vmem = spec(pltpu.VMEM)
    return pl.pallas_call(
        functools.partial(last_kernel, factor),
        in_specs=[vmem] * 3,
        out_specs=vmem,
        out_shape=jax.ShapeDtypeStruct((2 * W, width), F32),
        compiler_params=params(2),
        cost_estimate=pl.CostEstimate(flops=1 << 20, bytes_accessed=2 << 20, transcendentals=0),
    )(a, b, got)


def local(counts, row_marg, ctx_marg, discount, probes):
    power, shrink, total, inv_row, tail = context(ctx_marg, discount, row_marg)
    sent = prepare(1, counts, tail)
    received = [permute(sent[g], u_perm(NEAR[g])) for g in range(2)]
    total = total + permute(total, CORE_PERM)
    other = permute(total, ZL_PERM)
    kept, = prepare(0, counts)
    tile, y_part = forward(total, other, inv_row, power, shrink, kept, sent, probes)
    y_chip = (y_part + permute(y_part, CORE_PERM)).astype(BF16)
    y_own = (y_chip.astype(F32) + permute(y_chip, ZL_PERM).astype(F32)).astype(BF16)
    y_other = lax.optimization_barrier([permute(y_own, u_perm(NEAR[g])) for g in range(2)])

    def run(g, half, dtype):
        return back(total, other, power, shrink, y_own, y_other[g], tile, received[g], g, half, dtype)

    own, ends = [], []
    sends = [run(g, 1, BF16) for g in range(2)]
    for g in range(2):
        r2 = permute(sends[g], u_perm(FAR[g]))
        z = run(g, 0, F32)
        r3 = permute((z[4:8] + r2[4:8].astype(F32)).astype(BF16), v_perm(NEAR[g]))
        r4 = permute((z[2:4] + r2[2:4].astype(F32) + r3[2:4].astype(F32)).astype(BF16), v_perm(FAR[g]))
        kept = [z[k] + r2[k].astype(F32) + r3[k].astype(F32) + r4[k].astype(F32) for k in range(2)]
        own.append(kept[0])
        ends.append(kept[1].astype(BF16))
    r5 = permute(pair(*ends), ZH_PERM)
    factor = (counts.shape[0] * lax.axis_size("rows")) ** (-0.5)
    z_proj = last(*own, r5, factor)
    return (jnp.transpose(y_own), z_proj[None])


def solution(mesh):
    in_specs = (P("rows", "cols"), P("rows"), P("cols"), P("cols"), P("cols", None))
    out_specs = (P("rows", None), P("cols", "rows", None))
    return jax.shard_map(local, mesh=mesh, in_specs=in_specs, out_specs=out_specs, check_vma=False)
```

```python
import functools

import jax
import jax.numpy as jnp
from jax import lax
from jax.experimental import pallas as pl
from jax.experimental.pallas import tpu as pltpu
from jax.sharding import PartitionSpec as P

AXES = ("rows", "cols")
W = 256
STEP = 8
F32, BF16 = jnp.float32, jnp.bfloat16

NEAR, FAR = (1, 3), (3, 1)


def xor_perm(mask):
    pairs = []
    for d in range(128):
        r, zl, core = d >> 2, (d >> 1) & 1, d & 1
        dr, dzl, dcore = mask(core)
        pairs.append((d, ((r ^ dr) << 2) | ((zl ^ dzl) << 1) | (core ^ dcore)))
    return pairs


def u_perm(d):
    return xor_perm(lambda core: (d * (2 if core else 8), 0, 0))


def v_perm(d):
    return xor_perm(lambda core: (d * (8 if core else 2), 0, 0))


ZH_PERM = xor_perm(lambda core: (1, 0, 0))
ZL_PERM = xor_perm(lambda core: (0, 1, 0))
CORE_PERM = xor_perm(lambda core: (0, 0, 1))


def permute(a, perm):
    return lax.ppermute(a, AXES, perm)


def place():
    core = lax.rem(lax.axis_index("cols"), 2)
    return lax.axis_index("rows"), core


def block_of(r, core, g, d, e, k):
    return (r ^ (d * (8 - 6 * core) + e * (2 + 6 * core) + k)) * 2 + g


def slots(g, part):
    return [((NEAR[g] if part else 0) ^ (FAR[g] * i), e, k) for i in range(2) for k in (1, 0) for e in range(4)]


def params(mib):
    return pltpu.CompilerParams(vmem_limit_bytes=mib << 20)


def spec(space):
    return pl.BlockSpec(memory_space=space)


def context_kernel(all_ref, power_ref, shrink_ref, total_ref, inv_ref, tail_ref):
    power = jnp.exp(0.75 * jnp.log(all_ref[0:128, :].astype(F32)))
    power_ref[...] = 1.0 / power
    shrink_ref[...] = all_ref[128:256, :].astype(F32) * 0.25
    total_ref[...] = jnp.full((8, 128), jnp.sum(power), F32)
    wide = jnp.concatenate([all_ref[256:257, :], all_ref[257:258, :]], axis=1)
    inv_ref[...] = 1.0 / jnp.transpose(jnp.broadcast_to(wide.astype(F32), (128, W)))
    at = lax.broadcasted_iota(jnp.int32, (16, W), 0)
    low, mid, high = wide & 63, (wide >> 6) & 63, wide >> 12
    tail_ref[...] = jnp.where(at == 0, low, jnp.where(at == 1, mid, high)).astype(F32).astype(BF16)


def context(ctx_marg, discount, row_marg):
    square = jax.ShapeDtypeStruct((128, 128), F32)
    return pl.pallas_call(
        context_kernel,
        in_specs=[spec(pltpu.VMEM)],
        out_specs=[spec(pltpu.VMEM)] * 5,
        out_shape=(square, square, jax.ShapeDtypeStruct((8, 128), F32), jax.ShapeDtypeStruct((W, 128), F32),
                   jax.ShapeDtypeStruct((16, W), BF16)),
        compiler_params=params(2),
        cost_estimate=pl.CostEstimate(flops=1 << 18, bytes_accessed=1 << 18, transcendentals=1 << 15),
    )(jnp.concatenate([ctx_marg, discount, row_marg]).reshape(258, 128))


def prepare_kernel(part, *refs):
    if part == 1:
        tail_ref, counts_ref, *outs, in_ref, sem = refs
        for out_ref in outs:
            out_ref[16 * W:16 * W + 16, :] = tail_ref[...]
    else:
        counts_ref, kept_ref, in_ref, sem = refs
    r, core = place()

    def fetch(s):
        d, e, k = slots(s // 16, part)[s % 16]
        at = pl.multiple_of(block_of(r, core, s // 16, d, e, k) * W, W)
        return pltpu.make_async_copy(counts_ref.at[:, pl.ds(at, W)], in_ref.at[s], sem.at[s])

    for s in range(32):
        fetch(s).start()
    for s in range(32):
        fetch(s).wait()
        block = in_ref[s].astype(F32).astype(BF16)
        if part == 1:
            outs[s // 16][s % 16 * W:(s % 16 + 1) * W, :] = block
        else:
            kept_ref[s * W:(s + 1) * W, :] = block


def prepare(part, counts, *tail):
    rows = counts.shape[0]
    lengths = [16 * W + 16] * 2 if part else [32 * W]
    return pl.pallas_call(
        functools.partial(prepare_kernel, part),
        in_specs=[spec(pltpu.VMEM)] * part + [spec(pl.ANY)],
        out_specs=[spec(pltpu.VMEM)] * len(lengths),
        out_shape=[jax.ShapeDtypeStruct((n, W), BF16) for n in lengths],
        scratch_shapes=[pltpu.VMEM((32, rows, W), jnp.int32), pltpu.SemaphoreType.DMA((32,))],
        compiler_params=params(42),
        cost_estimate=pl.CostEstimate(flops=1 << 22, bytes_accessed=12 << 20, transcendentals=0),
    )(*tail, counts)


def tile_rows(counts, shrink, scale, inv_row):
    inv_row = jnp.concatenate([inv_row, inv_row], axis=1)
    excess = counts.astype(F32) - shrink
    return jnp.log(jnp.maximum(excess * scale * inv_row, 1.0)).astype(BF16)


def column_terms(ref, block):
    return jnp.concatenate([ref[pl.ds(2 * block, 1), :], ref[pl.ds(2 * block + 1, 1), :]], axis=1)


def whole_total(a_ref, b_ref):
    both = a_ref[0:1, :] + b_ref[0:1, :]
    return jnp.concatenate([both, both], axis=1)


def forward_kernel(total_ref, other_ref, inv_ref, power_ref, shrink_ref, kept_ref, sent_a, sent_b, probes_ref,
                   tile_ref, y_ref, acc_ref, work_ref):
    r, core = place()
    total = whole_total(total_ref, other_ref)
    rows = inv_ref.shape[0]
    acc_ref[...] = jnp.zeros_like(acc_ref)
    for g, sent_ref in enumerate((sent_a, sent_b)):
        for part in range(2):
            @pl.loop(0, 2)
            def _(i):
                sums = None
                for n, (d, e, k) in enumerate(slots(g, part)[:8]):
                    block = block_of(r, core, g, d ^ (FAR[g] * i), e, k)
                    at = pl.multiple_of(block * W, W)
                    shrink = column_terms(shrink_ref, block)
                    scale = column_terms(power_ref, block) * total
                    if part == 0:
                        source, base, out = kept_ref, (16 * g + 8 * i + n) * rows, tile_ref.at[16 * g + 8 * i + n]
                    else:
                        source, base, out = sent_ref, (8 * i + n) * rows, work_ref.at[n]
                    base = pl.multiple_of(base, rows)
                    for q in range(0, rows, 32):
                        out[q:q + 32, :] = tile_rows(source[pl.ds(base + q, 32), :], shrink, scale, inv_ref[q:q + 32, :])
                    term = jnp.dot(out[...], probes_ref[pl.ds(at, W), :], preferred_element_type=F32)
                    sums = term if sums is None else sums + term
                acc_ref[...] += sums
    y_ref[...] = jnp.transpose(acc_ref[...])


def forward(total, other, inv_row, power, shrink, kept, sent, probes):
    rows, width = inv_row.shape[0], probes.shape[1]
    vmem = spec(pltpu.VMEM)
    return pl.pallas_call(
        forward_kernel,
        in_specs=[vmem] * 9,
        out_specs=[vmem, vmem],
        scratch_shapes=[pltpu.VMEM((rows, width), F32), pltpu.VMEM((STEP, rows, W), BF16)],
        out_shape=(jax.ShapeDtypeStruct((32, rows, W), BF16), jax.ShapeDtypeStruct((width, rows), F32)),
        compiler_params=params(6),
        cost_estimate=pl.CostEstimate(flops=1 << 31, bytes_accessed=28 << 20, transcendentals=1 << 22),
    )(total, other, inv_row, power, shrink, kept, *sent, probes)


def other_kernel(group, total_ref, other_ref, power_ref, shrink_ref, count_ref, tile_ref, inv_ref):
    r, core = place()
    total = whole_total(total_ref, other_ref)
    rows = tile_ref.shape[1]
    tail = count_ref[16 * W:16 * W + 16, :].astype(F32)
    marg = tail[0:1, :] + tail[1:2, :] * 64.0 + tail[2:3, :] * 4096.0
    inv_ref[...] = 1.0 / jnp.transpose(jnp.broadcast_to(marg, (128, rows)))

    @pl.loop(0, 2)
    def _(i):
        for n, (d, e, k) in enumerate(slots(group, 0)[:8]):
            block = block_of(r, core, group, d ^ (FAR[group] * i), e, k)
            shrink = column_terms(shrink_ref, block)
            scale = column_terms(power_ref, block) * total
            s = 8 * i + n
            base = pl.multiple_of(s * rows, rows)
            for q in range(0, rows, 32):
                tile_ref[s, q:q + 32, :] = tile_rows(count_ref[pl.ds(base + q, 32), :], shrink, scale, inv_ref[q:q + 32, :])


def other_tile(group, total, other, power, shrink, received):
    vmem = spec(pltpu.VMEM)
    return pl.pallas_call(
        functools.partial(other_kernel, group),
        in_specs=[vmem] * 5,
        out_specs=vmem,
        scratch_shapes=[pltpu.VMEM((W, 128), F32)],
        out_shape=jax.ShapeDtypeStruct((16, W, W), BF16),
        compiler_params=params(4),
        cost_estimate=pl.CostEstimate(flops=1 << 24, bytes_accessed=4 << 20, transcendentals=1 << 20),
    )(total, other, power, shrink, received)


def back_kernel(base, half, y_own_ref, y_other_ref, own_ref, other_ref, *outs):
    for n in range(8):
        out = jnp.dot(y_own_ref[...], own_ref[base + half * 8 + n], preferred_element_type=F32)
        out = out + jnp.dot(y_other_ref[...], other_ref[half * 8 + n], preferred_element_type=F32)
        outs[n // 4][n % 4] = out.astype(outs[0].dtype)


def back(group, half, y_own, y_other, own, other, dtype):
    vmem = spec(pltpu.VMEM)
    return pl.pallas_call(
        functools.partial(back_kernel, group * 16, half),
        in_specs=[vmem] * 4,
        out_specs=[vmem] * 2,
        out_shape=[jax.ShapeDtypeStruct((4, y_own.shape[0], W), dtype)] * 2,
        compiler_params=params(4),
        cost_estimate=pl.CostEstimate(flops=1 << 29, bytes_accessed=4 << 20, transcendentals=0),
    )(y_own, y_other, own, other)


def pack_kernel(z_a, r_a, z_b, r_b, own_ref, *outs):
    for g, (z_ref, r_ref) in enumerate(((z_a, r_a), (z_b, r_b))):
        for e in range(4):
            total = z_ref[e] + r_ref[e].astype(F32)
            if e == 0:
                own_ref[g] = total
            else:
                outs[e - 1][g] = total.astype(BF16)


def pack(z, r):
    vmem = spec(pltpu.VMEM)
    width = z[0].shape[1]
    return pl.pallas_call(
        pack_kernel,
        in_specs=[vmem] * 4,
        out_specs=[vmem] * 4,
        out_shape=[jax.ShapeDtypeStruct((2, width, W), F32)] + [jax.ShapeDtypeStruct((2, width, W), BF16)] * 3,
        compiler_params=params(4),
        cost_estimate=pl.CostEstimate(flops=1 << 21, bytes_accessed=4 << 20, transcendentals=0),
    )(z[0], r[0], z[1], r[1])


def fold_kernel(own_ref, a_ref, b_ref, c_ref, out_ref):
    for g in range(2):
        total = own_ref[g] + a_ref[g].astype(F32) + b_ref[g].astype(F32) + c_ref[g].astype(F32)
        out_ref[g] = total.astype(out_ref.dtype)


def fold(own, got, dtype):
    vmem = spec(pltpu.VMEM)
    return pl.pallas_call(
        fold_kernel,
        in_specs=[vmem] * 4,
        out_specs=vmem,
        out_shape=jax.ShapeDtypeStruct(own.shape, dtype),
        compiler_params=params(4),
        cost_estimate=pl.CostEstimate(flops=1 << 20, bytes_accessed=2 << 20, transcendentals=0),
    )(own, *got)


def last_kernel(factor, own_ref, got_ref, z_ref):
    for g in range(2):
        z_ref[g * W:(g + 1) * W, :] = jnp.transpose(own_ref[g] + got_ref[g].astype(F32)) * factor


def last(own, got, factor):
    width = own.shape[1]
    vmem = spec(pltpu.VMEM)
    return pl.pallas_call(
        functools.partial(last_kernel, factor),
        in_specs=[vmem] * 2,
        out_specs=vmem,
        out_shape=jax.ShapeDtypeStruct((2 * W, width), F32),
        compiler_params=params(4),
        cost_estimate=pl.CostEstimate(flops=1 << 20, bytes_accessed=2 << 20, transcendentals=0),
    )(own, got)


def local(counts, row_marg, ctx_marg, discount, probes):
    power, shrink, total, inv_row, tail = context(ctx_marg, discount, row_marg)
    sent = prepare(1, counts, tail)
    received = [permute(sent[g], u_perm(NEAR[g])) for g in range(2)]
    total = total + permute(total, CORE_PERM)
    other = permute(total, ZL_PERM)
    kept, = prepare(0, counts)
    tile, y_part = forward(total, other, inv_row, power, shrink, kept, sent, probes)
    y_chip = (y_part + permute(y_part, CORE_PERM)).astype(BF16)
    y_own = (y_chip.astype(F32) + permute(y_chip, ZL_PERM).astype(F32)).astype(BF16)
    y_other = [permute(y_own, u_perm(NEAR[g])) for g in range(2)]

    tiles = [other_tile(g, total, other, power, shrink, received[g]) for g in range(2)]
    y_other, tiles = lax.optimization_barrier((y_other, tiles))
    sends = [back(g, 1, y_own, y_other[g], tile, tiles[g], BF16) for g in range(2)]
    r2 = [[permute(sends[g][c], u_perm(FAR[g])) for g in range(2)] for c in range(2)]
    z = [back(g, 0, y_own, y_other[g], tile, tiles[g], F32) for g in range(2)]
    ended = []
    for c, dtype in enumerate((BF16, F32)):
        own, *out = pack([z[g][c] for g in range(2)], r2[c])
        ended.append(fold(own, [permute(out[e - 1], v_perm(e)) for e in (2, 1, 3)], dtype))
    factor = (counts.shape[0] * lax.axis_size("rows")) ** (-0.5)
    z_proj = last(ended[1], permute(ended[0], ZH_PERM), factor)
    return (jnp.transpose(y_own), z_proj[None])


def solution(mesh):
    in_specs = (P("rows", "cols"), P("rows"), P("cols"), P("cols"), P("cols", None))
    out_specs = (P("rows", None), P("cols", "rows", None))
    return jax.shard_map(local, mesh=mesh, in_specs=in_specs, out_specs=out_specs, check_vma=False)
```

```python
import functools

import jax
import jax.numpy as jnp
from jax import lax
from jax.experimental import pallas as pl
from jax.experimental.pallas import tpu as pltpu
from jax.sharding import PartitionSpec as P

AXES = ("rows", "cols")
W = 256
STEP = 8
F32, BF16 = jnp.float32, jnp.bfloat16

NEAR, FAR = (3, 1), (1, 3)


def xor_perm(mask):
    pairs = []
    for d in range(128):
        r, zl, core = d >> 2, (d >> 1) & 1, d & 1
        dr, dzl, dcore = mask(core)
        pairs.append((d, ((r ^ dr) << 2) | ((zl ^ dzl) << 1) | (core ^ dcore)))
    return pairs


def u_perm(d):
    return xor_perm(lambda core: (d * (2 if core else 8), 0, 0))


def v_perm(d):
    return xor_perm(lambda core: (d * (8 if core else 2), 0, 0))


ZH_PERM = xor_perm(lambda core: (1, 0, 0))
ZL_PERM = xor_perm(lambda core: (0, 1, 0))
CORE_PERM = xor_perm(lambda core: (0, 0, 1))


def permute(a, perm):
    return lax.ppermute(a, AXES, perm)


def place():
    core = lax.rem(lax.axis_index("cols"), 2)
    return lax.axis_index("rows"), core


def block_of(r, core, g, d, e, k):
    return (r ^ (d * (8 - 6 * core) + e * (2 + 6 * core) + k)) * 2 + g


def slots(g, part):
    return [((NEAR[g] if part else 0) ^ (FAR[g] * i), e, k) for i in range(2) for k in (1, 0) for e in range(4)]


def params(mib):
    return pltpu.CompilerParams(vmem_limit_bytes=mib << 20)


def spec(space):
    return pl.BlockSpec(memory_space=space)


def context_kernel(all_ref, power_ref, shrink_ref, total_ref, inv_ref, tail_ref):
    power = jnp.exp(0.75 * jnp.log(all_ref[0:128, :].astype(F32)))
    power_ref[...] = 1.0 / power
    shrink_ref[...] = all_ref[128:256, :].astype(F32) * 0.25
    total_ref[...] = jnp.full((8, 128), jnp.sum(power), F32)
    wide = jnp.concatenate([all_ref[256:257, :], all_ref[257:258, :]], axis=1)
    inv_ref[...] = 1.0 / jnp.transpose(jnp.broadcast_to(wide.astype(F32), (128, W)))
    at = lax.broadcasted_iota(jnp.int32, (16, W), 0)
    low, mid, high = wide & 63, (wide >> 6) & 63, wide >> 12
    tail_ref[...] = jnp.where(at == 0, low, jnp.where(at == 1, mid, high)).astype(F32).astype(BF16)


def context(ctx_marg, discount, row_marg):
    square = jax.ShapeDtypeStruct((128, 128), F32)
    return pl.pallas_call(
        context_kernel,
        in_specs=[spec(pltpu.VMEM)],
        out_specs=[spec(pltpu.VMEM)] * 5,
        out_shape=(square, square, jax.ShapeDtypeStruct((8, 128), F32), jax.ShapeDtypeStruct((W, 128), F32),
                   jax.ShapeDtypeStruct((16, W), BF16)),
        compiler_params=params(2),
        cost_estimate=pl.CostEstimate(flops=1 << 18, bytes_accessed=1 << 18, transcendentals=1 << 15),
    )(jnp.concatenate([ctx_marg, discount, row_marg]).reshape(258, 128))


def fetch_block(counts_ref, in_ref, sem, g, part, s, i=0):
    r, core = place()
    d, e, k = slots(g, part)[s]
    at = pl.multiple_of(block_of(r, core, g, d ^ (FAR[g] * i), e, k) * W, W)
    return pltpu.make_async_copy(counts_ref.at[:, pl.ds(at, W)], in_ref.at[s + 8 * i], sem.at[s + 8 * i])


def prepare_kernel(part, *refs):
    if part == 1:
        tail_ref, counts_ref, *outs, in_a, in_b, sem_a, sem_b = refs
        bufs = ((in_a, sem_a), (in_b, sem_b))
    else:
        counts_ref, *outs, in_a, sem_a = refs
        bufs = ((in_a, sem_a),)
    copies = [(g, s) for g in range(len(outs)) for s in range(16)]
    for g, s in copies:
        fetch_block(counts_ref, *bufs[g], g, part, s).start()
    if part == 1:
        for out_ref in outs:
            out_ref[16 * W:16 * W + 16, :] = tail_ref[...]
    for g, s in copies:
        fetch_block(counts_ref, *bufs[g], g, part, s).wait()
        outs[g][s * W:(s + 1) * W, :] = bufs[g][0][s].astype(F32).astype(BF16)


def prepare(part, counts, *tail):
    rows = counts.shape[0]
    n = 1 + part
    return pl.pallas_call(
        functools.partial(prepare_kernel, part),
        in_specs=[spec(pltpu.VMEM)] * part + [spec(pl.ANY)],
        out_specs=[spec(pltpu.VMEM)] * n,
        out_shape=[jax.ShapeDtypeStruct((16 * W + 16 * part, W), BF16)] * n,
        scratch_shapes=[pltpu.VMEM((16, rows, W), jnp.int32)] * n + [pltpu.SemaphoreType.DMA((16,))] * n,
        compiler_params=params(38),
        cost_estimate=pl.CostEstimate(flops=1 << 22, bytes_accessed=n * (6 << 20), transcendentals=0),
    )(*tail, counts)


def tile_rows(counts, shrink, scale, inv_row):
    inv_row = jnp.concatenate([inv_row, inv_row], axis=1)
    excess = counts.astype(F32) - shrink
    return jnp.log(jnp.maximum(excess * scale * inv_row, 1.0)).astype(BF16)


def column_terms(ref, block):
    return jnp.concatenate([ref[pl.ds(2 * block, 1), :], ref[pl.ds(2 * block + 1, 1), :]], axis=1)


def whole_total(a_ref, b_ref):
    both = a_ref[0:1, :] + b_ref[0:1, :]
    return jnp.concatenate([both, both], axis=1)


def forward_kernel(total_ref, other_ref, inv_ref, power_ref, shrink_ref, sent_a, sent_b, kept_a, probes_ref, counts_ref,
                   tile_ref, y_ref, acc_ref, work_ref, in_ref, sem):
    r, core = place()
    total = whole_total(total_ref, other_ref)
    rows = inv_ref.shape[0]
    for s in range(16):
        fetch_block(counts_ref, in_ref, sem, 1, 0, s).start()
    acc_ref[...] = jnp.zeros_like(acc_ref)
    for part, g, blocks in ((1, 0, sent_a), (1, 1, sent_b), (0, 0, kept_a), (0, 1, None)):
        @pl.loop(0, 2)
        def _(i):
            sums = None
            if blocks is None:
                for n in range(8):
                    fetch_block(counts_ref, in_ref, sem, g, part, n, i).wait()
            for n, (d, e, k) in enumerate(slots(g, part)[:8]):
                block = block_of(r, core, g, d ^ (FAR[g] * i), e, k)
                at = pl.multiple_of(block * W, W)
                shrink = column_terms(shrink_ref, block)
                scale = column_terms(power_ref, block) * total
                if blocks is None:
                    source = in_ref.at[8 * i + n]
                else:
                    source = blocks.at[pl.ds(pl.multiple_of((8 * i + n) * rows, rows), rows)]
                out = work_ref.at[n] if part else tile_ref.at[16 * g + 8 * i + n]
                for q in range(0, rows, 32):
                    out[q:q + 32, :] = tile_rows(source[q:q + 32, :], shrink, scale, inv_ref[q:q + 32, :])
                term = jnp.dot(out[...], probes_ref[pl.ds(at, W), :], preferred_element_type=F32)
                sums = term if sums is None else sums + term
            acc_ref[...] += sums
    y_ref[...] = jnp.transpose(acc_ref[...])


def forward(total, other, inv_row, power, shrink, sent, kept, probes, counts):
    rows, width = inv_row.shape[0], probes.shape[1]
    vmem = spec(pltpu.VMEM)
    return pl.pallas_call(
        forward_kernel,
        in_specs=[vmem] * 9 + [spec(pl.ANY)],
        out_specs=[vmem, vmem],
        scratch_shapes=[
            pltpu.VMEM((rows, width), F32),
            pltpu.VMEM((STEP, rows, W), BF16),
            pltpu.VMEM((16, rows, W), jnp.int32),
            pltpu.SemaphoreType.DMA((16,)),
        ],
        out_shape=(jax.ShapeDtypeStruct((32, rows, W), BF16), jax.ShapeDtypeStruct((width, rows), F32)),
        compiler_params=params(30),
        cost_estimate=pl.CostEstimate(flops=1 << 31, bytes_accessed=28 << 20, transcendentals=1 << 22),
    )(total, other, inv_row, power, shrink, *sent, kept, probes, counts)


def other_kernel(group, total_ref, other_ref, power_ref, shrink_ref, count_ref, tile_ref, inv_ref):
    r, core = place()
    total = whole_total(total_ref, other_ref)
    rows = tile_ref.shape[1]
    tail = count_ref[16 * W:16 * W + 16, :].astype(F32)
    marg = tail[0:1, :] + tail[1:2, :] * 64.0 + tail[2:3, :] * 4096.0
    inv_ref[...] = 1.0 / jnp.transpose(jnp.broadcast_to(marg, (128, rows)))

    @pl.loop(0, 2)
    def _(i):
        for n, (d, e, k) in enumerate(slots(group, 0)[:8]):
            block = block_of(r, core, group, d ^ (FAR[group] * i), e, k)
            shrink = column_terms(shrink_ref, block)
            scale = column_terms(power_ref, block) * total
            s = 8 * i + n
            base = pl.multiple_of(s * rows, rows)
            for q in range(0, rows, 32):
                tile_ref[s, q:q + 32, :] = tile_rows(count_ref[pl.ds(base + q, 32), :], shrink, scale, inv_ref[q:q + 32, :])


def other_tile(group, total, other, power, shrink, received):
    vmem = spec(pltpu.VMEM)
    return pl.pallas_call(
        functools.partial(other_kernel, group),
        in_specs=[vmem] * 5,
        out_specs=vmem,
        scratch_shapes=[pltpu.VMEM((W, 128), F32)],
        out_shape=jax.ShapeDtypeStruct((16, W, W), BF16),
        compiler_params=params(4),
        cost_estimate=pl.CostEstimate(flops=1 << 24, bytes_accessed=4 << 20, transcendentals=1 << 20),
    )(total, other, power, shrink, received)


def back_kernel(base, half, y_own_ref, y_other_ref, own_ref, other_ref, *outs):
    for n in range(8):
        out = jnp.dot(y_own_ref[...], own_ref[base + half * 8 + n], preferred_element_type=F32)
        out = out + jnp.dot(y_other_ref[...], other_ref[half * 8 + n], preferred_element_type=F32)
        outs[n // 4][n % 4] = out.astype(outs[0].dtype)


def back(group, half, y_own, y_other, own, other, dtype):
    vmem = spec(pltpu.VMEM)
    return pl.pallas_call(
        functools.partial(back_kernel, group * 16, half),
        in_specs=[vmem] * 4,
        out_specs=[vmem] * 2,
        out_shape=[jax.ShapeDtypeStruct((4, y_own.shape[0], W), dtype)] * 2,
        compiler_params=params(4),
        cost_estimate=pl.CostEstimate(flops=1 << 29, bytes_accessed=4 << 20, transcendentals=0),
    )(y_own, y_other, own, other)


def pack_kernel(z_a, r_a, z_b, r_b, own_ref, *outs):
    for g, (z_ref, r_ref) in enumerate(((z_a, r_a), (z_b, r_b))):
        for e in range(4):
            total = z_ref[e] + r_ref[e].astype(F32)
            if e == 0:
                own_ref[g] = total
            else:
                outs[e - 1][g] = total.astype(BF16)


def pack(z, r):
    vmem = spec(pltpu.VMEM)
    width = z[0].shape[1]
    return pl.pallas_call(
        pack_kernel,
        in_specs=[vmem] * 4,
        out_specs=[vmem] * 4,
        out_shape=[jax.ShapeDtypeStruct((2, width, W), F32)] + [jax.ShapeDtypeStruct((2, width, W), BF16)] * 3,
        compiler_params=params(4),
        cost_estimate=pl.CostEstimate(flops=1 << 21, bytes_accessed=4 << 20, transcendentals=0),
    )(z[0], r[0], z[1], r[1])


def fold_kernel(own_ref, a_ref, b_ref, c_ref, out_ref):
    for g in range(2):
        total = own_ref[g] + a_ref[g].astype(F32) + b_ref[g].astype(F32) + c_ref[g].astype(F32)
        out_ref[g] = total.astype(out_ref.dtype)


def fold(own, got, dtype):
    vmem = spec(pltpu.VMEM)
    return pl.pallas_call(
        fold_kernel,
        in_specs=[vmem] * 4,
        out_specs=vmem,
        out_shape=jax.ShapeDtypeStruct(own.shape, dtype),
        compiler_params=params(4),
        cost_estimate=pl.CostEstimate(flops=1 << 20, bytes_accessed=2 << 20, transcendentals=0),
    )(own, *got)


def last_kernel(factor, own_ref, got_ref, z_ref):
    for g in range(2):
        z_ref[g * W:(g + 1) * W, :] = jnp.transpose(own_ref[g] + got_ref[g].astype(F32)) * factor


def last(own, got, factor):
    width = own.shape[1]
    vmem = spec(pltpu.VMEM)
    return pl.pallas_call(
        functools.partial(last_kernel, factor),
        in_specs=[vmem] * 2,
        out_specs=vmem,
        out_shape=jax.ShapeDtypeStruct((2 * W, width), F32),
        compiler_params=params(4),
        cost_estimate=pl.CostEstimate(flops=1 << 20, bytes_accessed=2 << 20, transcendentals=0),
    )(own, got)


def local(counts, row_marg, ctx_marg, discount, probes):
    power, shrink, total, inv_row, tail = context(ctx_marg, discount, row_marg)
    sent = prepare(1, counts, tail)
    total = total + permute(total, CORE_PERM)
    sent, total = lax.optimization_barrier((sent, total))
    received = [permute(sent[g], u_perm(NEAR[g])) for g in range(2)]
    other = permute(total, ZL_PERM)
    kept, = prepare(0, counts)
    tile, y_part = forward(total, other, inv_row, power, shrink, sent, kept, probes, counts)
    y_chip = (y_part + permute(y_part, CORE_PERM)).astype(BF16)
    y_own = (y_chip.astype(F32) + permute(y_chip, ZL_PERM).astype(F32)).astype(BF16)
    y_other = [permute(y_own, u_perm(NEAR[g])) for g in range(2)]

    tiles = [other_tile(g, total, other, power, shrink, received[g]) for g in range(2)]
    y_other, tiles = zip(*[lax.optimization_barrier((y_other[g], tiles[g])) for g in range(2)])
    sends = [back(g, 1, y_own, y_other[g], tile, tiles[g], BF16) for g in range(2)]
    r2 = [[permute(sends[g][c], u_perm(FAR[g])) for g in range(2)] for c in range(2)]
    z = [back(g, 0, y_own, y_other[g], tile, tiles[g], F32) for g in range(2)]
    ended = []
    for c, dtype in enumerate((BF16, F32)):
        own, *out = pack([z[g][c] for g in range(2)], r2[c])
        ended.append(fold(own, [permute(out[e - 1], v_perm(e)) for e in (3, 1, 2)], dtype))
    factor = (counts.shape[0] * lax.axis_size("rows")) ** (-0.5)
    z_proj = last(ended[1], permute(ended[0], ZH_PERM), factor)
    return (jnp.transpose(y_own), z_proj[None])


def solution(mesh):
    in_specs = (P("rows", "cols"), P("rows"), P("cols"), P("cols"), P("cols", None))
    out_specs = (P("rows", None), P("cols", "rows", None))
    return jax.shard_map(local, mesh=mesh, in_specs=in_specs, out_specs=out_specs, check_vma=False)
```

```python
import functools

import jax
import jax.numpy as jnp
from jax import lax
from jax.experimental import pallas as pl
from jax.experimental.pallas import tpu as pltpu
from jax.sharding import PartitionSpec as P

AXES = ("rows", "cols")
W = 256
STEP = 8
F32, BF16 = jnp.float32, jnp.bfloat16

NEAR, FAR = (3, 1), (1, 3)


def xor_perm(mask):
    pairs = []
    for d in range(128):
        r, zl, core = d >> 2, (d >> 1) & 1, d & 1
        dr, dzl, dcore = mask(core)
        pairs.append((d, ((r ^ dr) << 2) | ((zl ^ dzl) << 1) | (core ^ dcore)))
    return pairs


def u_perm(d):
    return xor_perm(lambda core: (d * (2 if core else 8), 0, 0))


def v_perm(d):
    return xor_perm(lambda core: (d * (8 if core else 2), 0, 0))


ZH_PERM = xor_perm(lambda core: (1, 0, 0))
ZL_PERM = xor_perm(lambda core: (0, 1, 0))
CORE_PERM = xor_perm(lambda core: (0, 0, 1))


def permute(a, perm):
    return lax.ppermute(a, AXES, perm)


def place():
    core = lax.rem(lax.axis_index("cols"), 2)
    return lax.axis_index("rows"), core


def block_of(r, core, g, d, e, k):
    return (r ^ (d * (8 - 6 * core) + e * (2 + 6 * core) + k)) * 2 + g


def slots(g, part):
    return [((NEAR[g] if part else 0) ^ (FAR[g] * i), e, k) for i in range(2) for k in (1, 0) for e in range(4)]


def params(mib):
    return pltpu.CompilerParams(vmem_limit_bytes=mib << 20)


def spec(space):
    return pl.BlockSpec(memory_space=space)


def context_kernel(all_ref, power_ref, shrink_ref, total_ref, inv_ref, tail_ref):
    power = jnp.exp(0.75 * jnp.log(all_ref[0:128, :].astype(F32)))
    power_ref[...] = 1.0 / power
    shrink_ref[...] = all_ref[128:256, :].astype(F32) * 0.25
    total_ref[...] = jnp.full((8, 128), jnp.sum(power), F32)
    wide = jnp.concatenate([all_ref[256:257, :], all_ref[257:258, :]], axis=1)
    inv_ref[...] = 1.0 / jnp.transpose(jnp.broadcast_to(wide.astype(F32), (128, W)))
    at = lax.broadcasted_iota(jnp.int32, (16, W), 0)
    low, mid, high = wide & 63, (wide >> 6) & 63, wide >> 12
    tail_ref[...] = jnp.where(at == 0, low, jnp.where(at == 1, mid, high)).astype(F32).astype(BF16)


def context(ctx_marg, discount, row_marg):
    square = jax.ShapeDtypeStruct((128, 128), F32)
    return pl.pallas_call(
        context_kernel,
        in_specs=[spec(pltpu.VMEM)],
        out_specs=[spec(pltpu.VMEM)] * 5,
        out_shape=(square, square, jax.ShapeDtypeStruct((8, 128), F32), jax.ShapeDtypeStruct((W, 128), F32),
                   jax.ShapeDtypeStruct((16, W), BF16)),
        compiler_params=params(2),
        cost_estimate=pl.CostEstimate(flops=1 << 18, bytes_accessed=1 << 18, transcendentals=1 << 15),
    )(jnp.concatenate([ctx_marg, discount, row_marg]).reshape(258, 128))


def fetch_block(counts_ref, in_ref, sem, g, part, s, i=0):
    r, core = place()
    d, e, k = slots(g, part)[s]
    at = pl.multiple_of(block_of(r, core, g, d ^ (FAR[g] * i), e, k) * W, W)
    return pltpu.make_async_copy(counts_ref.at[:, pl.ds(at, W)], in_ref.at[s + 8 * i], sem.at[s + 8 * i])


def prepare_kernel(part, *refs):
    if part == 1:
        tail_ref, counts_ref, *outs, in_a, in_b, sem_a, sem_b = refs
        bufs = ((in_a, sem_a), (in_b, sem_b))
    else:
        counts_ref, *outs, in_a, sem_a = refs
        bufs = ((in_a, sem_a),)
    copies = [(g, s) for g in range(len(outs)) for s in range(16)]
    for g, s in copies:
        fetch_block(counts_ref, *bufs[g], g, part, s).start()
    if part == 1:
        for out_ref in outs:
            out_ref[16 * W:16 * W + 16, :] = tail_ref[...]
    for g, s in copies:
        fetch_block(counts_ref, *bufs[g], g, part, s).wait()
        outs[g][s * W:(s + 1) * W, :] = bufs[g][0][s].astype(F32).astype(BF16)


def prepare(part, counts, *tail):
    rows = counts.shape[0]
    n = 1 + part
    return pl.pallas_call(
        functools.partial(prepare_kernel, part),
        in_specs=[spec(pltpu.VMEM)] * part + [spec(pl.ANY)],
        out_specs=[spec(pltpu.VMEM)] * n,
        out_shape=[jax.ShapeDtypeStruct((16 * W + 16 * part, W), BF16)] * n,
        scratch_shapes=[pltpu.VMEM((16, rows, W), jnp.int32)] * n + [pltpu.SemaphoreType.DMA((16,))] * n,
        compiler_params=params(38),
        cost_estimate=pl.CostEstimate(flops=1 << 22, bytes_accessed=n * (6 << 20), transcendentals=0),
    )(*tail, counts)


def tile_rows(counts, shrink, scale, inv_row):
    inv_row = jnp.concatenate([inv_row, inv_row], axis=1)
    excess = counts.astype(F32) - shrink
    return jnp.log(jnp.maximum(excess * scale * inv_row, 1.0)).astype(BF16)


def column_terms(ref, block):
    return jnp.concatenate([ref[pl.ds(2 * block, 1), :], ref[pl.ds(2 * block + 1, 1), :]], axis=1)


def whole_total(a_ref, b_ref):
    both = a_ref[0:1, :] + b_ref[0:1, :]
    return jnp.concatenate([both, both], axis=1)


def forward_kernel(total_ref, other_ref, inv_ref, power_ref, shrink_ref, sent_a, sent_b, kept_a, probes_ref, counts_ref,
                   tile_ref, y_ref, acc_ref, work_ref, in_ref, sem):
    r, core = place()
    total = whole_total(total_ref, other_ref)
    rows = inv_ref.shape[0]
    for s in range(16):
        fetch_block(counts_ref, in_ref, sem, 1, 0, s).start()
    acc_ref[...] = jnp.zeros_like(acc_ref)
    for part, g, blocks in ((1, 0, sent_a), (1, 1, sent_b), (0, 0, kept_a), (0, 1, None)):
        @pl.loop(0, 2)
        def _(i):
            sums = None
            if blocks is None:
                for n in range(8):
                    fetch_block(counts_ref, in_ref, sem, g, part, n, i).wait()
            for n, (d, e, k) in enumerate(slots(g, part)[:8]):
                block = block_of(r, core, g, d ^ (FAR[g] * i), e, k)
                at = pl.multiple_of(block * W, W)
                shrink = column_terms(shrink_ref, block)
                scale = column_terms(power_ref, block) * total
                if blocks is None:
                    source = in_ref.at[8 * i + n]
                else:
                    source = blocks.at[pl.ds(pl.multiple_of((8 * i + n) * rows, rows), rows)]
                out = work_ref.at[n] if part else tile_ref.at[16 * g + 8 * i + n]
                for q in range(0, rows, 32):
                    out[q:q + 32, :] = tile_rows(source[q:q + 32, :], shrink, scale, inv_ref[q:q + 32, :])
                term = jnp.dot(out[...], probes_ref[pl.ds(at, W), :], preferred_element_type=F32)
                sums = term if sums is None else sums + term
            acc_ref[...] += sums
    y_ref[...] = jnp.transpose(acc_ref[...])


def forward(total, other, inv_row, power, shrink, sent, kept, probes, counts):
    rows, width = inv_row.shape[0], probes.shape[1]
    vmem = spec(pltpu.VMEM)
    return pl.pallas_call(
        forward_kernel,
        in_specs=[vmem] * 9 + [spec(pl.ANY)],
        out_specs=[vmem, vmem],
        scratch_shapes=[
            pltpu.VMEM((rows, width), F32),
            pltpu.VMEM((STEP, rows, W), BF16),
            pltpu.VMEM((16, rows, W), jnp.int32),
            pltpu.SemaphoreType.DMA((16,)),
        ],
        out_shape=(jax.ShapeDtypeStruct((32, rows, W), BF16), jax.ShapeDtypeStruct((width, rows), F32)),
        compiler_params=params(30),
        cost_estimate=pl.CostEstimate(flops=1 << 31, bytes_accessed=28 << 20, transcendentals=1 << 22),
    )(total, other, inv_row, power, shrink, *sent, kept, probes, counts)


def other_kernel(group, total_ref, other_ref, power_ref, shrink_ref, count_ref, tile_ref, inv_ref):
    r, core = place()
    total = whole_total(total_ref, other_ref)
    rows = tile_ref.shape[1]
    tail = count_ref[16 * W:16 * W + 16, :].astype(F32)
    marg = tail[0:1, :] + tail[1:2, :] * 64.0 + tail[2:3, :] * 4096.0
    inv_ref[...] = 1.0 / jnp.transpose(jnp.broadcast_to(marg, (128, rows)))

    @pl.loop(0, 2)
    def _(i):
        for n, (d, e, k) in enumerate(slots(group, 0)[:8]):
            block = block_of(r, core, group, d ^ (FAR[group] * i), e, k)
            shrink = column_terms(shrink_ref, block)
            scale = column_terms(power_ref, block) * total
            s = 8 * i + n
            base = pl.multiple_of(s * rows, rows)
            for q in range(0, rows, 32):
                tile_ref[s, q:q + 32, :] = tile_rows(count_ref[pl.ds(base + q, 32), :], shrink, scale, inv_ref[q:q + 32, :])


def other_tile(group, total, other, power, shrink, received):
    vmem = spec(pltpu.VMEM)
    return pl.pallas_call(
        functools.partial(other_kernel, group),
        in_specs=[vmem] * 5,
        out_specs=vmem,
        scratch_shapes=[pltpu.VMEM((W, 128), F32)],
        out_shape=jax.ShapeDtypeStruct((16, W, W), BF16),
        compiler_params=params(4),
        cost_estimate=pl.CostEstimate(flops=1 << 24, bytes_accessed=4 << 20, transcendentals=1 << 20),
    )(total, other, power, shrink, received)


def back_kernel(base, half, y_own_ref, y_other_ref, own_ref, other_ref, *outs):
    for n in range(8):
        out = jnp.dot(y_own_ref[...], own_ref[base + half * 8 + n], preferred_element_type=F32)
        out = out + jnp.dot(y_other_ref[...], other_ref[half * 8 + n], preferred_element_type=F32)
        outs[n // 4][n % 4] = out.astype(outs[0].dtype)


def back(group, half, y_own, y_other, own, other, dtype):
    vmem = spec(pltpu.VMEM)
    return pl.pallas_call(
        functools.partial(back_kernel, group * 16, half),
        in_specs=[vmem] * 4,
        out_specs=[vmem] * 2,
        out_shape=[jax.ShapeDtypeStruct((4, y_own.shape[0], W), dtype)] * 2,
        compiler_params=params(4),
        cost_estimate=pl.CostEstimate(flops=1 << 29, bytes_accessed=4 << 20, transcendentals=0),
    )(y_own, y_other, own, other)


def pack_kernel(z_a, r_a, z_b, r_b, own_ref, *outs):
    for g, (z_ref, r_ref) in enumerate(((z_a, r_a), (z_b, r_b))):
        for e in range(4):
            total = z_ref[e] + r_ref[e].astype(F32)
            if e == 0:
                own_ref[g] = total
            else:
                outs[e - 1][g] = total.astype(BF16)


def pack(z, r):
    vmem = spec(pltpu.VMEM)
    width = z[0].shape[1]
    return pl.pallas_call(
        pack_kernel,
        in_specs=[vmem] * 4,
        out_specs=[vmem] * 4,
        out_shape=[jax.ShapeDtypeStruct((2, width, W), F32)] + [jax.ShapeDtypeStruct((2, width, W), BF16)] * 3,
        compiler_params=params(4),
        cost_estimate=pl.CostEstimate(flops=1 << 21, bytes_accessed=4 << 20, transcendentals=0),
    )(z[0], r[0], z[1], r[1])


def fold_kernel(own_ref, a_ref, b_ref, c_ref, out_ref):
    for g in range(2):
        total = own_ref[g] + a_ref[g].astype(F32) + b_ref[g].astype(F32) + c_ref[g].astype(F32)
        out_ref[g] = (jnp.transpose(total) if out_ref.dtype == F32 else total).astype(out_ref.dtype)


def fold(own, got, dtype):
    vmem = spec(pltpu.VMEM)
    return pl.pallas_call(
        fold_kernel,
        in_specs=[vmem] * 4,
        out_specs=vmem,
        out_shape=jax.ShapeDtypeStruct(own.shape, dtype),
        compiler_params=params(4),
        cost_estimate=pl.CostEstimate(flops=1 << 20, bytes_accessed=2 << 20, transcendentals=0),
    )(own, *got)


def last_kernel(factor, own_ref, got_ref, z_ref):
    for g in range(2):
        z_ref[g * W:(g + 1) * W, :] = (own_ref[g] + jnp.transpose(got_ref[g].astype(F32))) * factor


def last(own, got, factor):
    width = own.shape[1]
    vmem = spec(pltpu.VMEM)
    return pl.pallas_call(
        functools.partial(last_kernel, factor),
        in_specs=[vmem] * 2,
        out_specs=vmem,
        out_shape=jax.ShapeDtypeStruct((2 * W, width), F32),
        compiler_params=params(4),
        cost_estimate=pl.CostEstimate(flops=1 << 20, bytes_accessed=2 << 20, transcendentals=0),
    )(own, got)


def local(counts, row_marg, ctx_marg, discount, probes):
    power, shrink, total, inv_row, tail = context(ctx_marg, discount, row_marg)
    sent = prepare(1, counts, tail)
    total = total + permute(total, CORE_PERM)
    sent, total = lax.optimization_barrier((sent, total))
    received = [permute(sent[g], u_perm(NEAR[g])) for g in range(2)]
    other = permute(total, ZL_PERM)
    kept, = prepare(0, counts)
    tile, y_part = forward(total, other, inv_row, power, shrink, sent, kept, probes, counts)
    y_chip = (y_part + permute(y_part, CORE_PERM)).astype(BF16)
    y_own = (y_chip.astype(F32) + permute(y_chip, ZL_PERM).astype(F32)).astype(BF16)
    y_other = [permute(y_own, u_perm(NEAR[g])) for g in range(2)]

    tiles = [other_tile(g, total, other, power, shrink, received[g]) for g in range(2)]
    y_other, tiles = zip(*[lax.optimization_barrier((y_other[g], tiles[g])) for g in range(2)])
    sends = [back(g, 1, y_own, y_other[g], tile, tiles[g], BF16) for g in range(2)]
    r2 = [[permute(sends[g][c], u_perm(FAR[g])) for g in range(2)] for c in range(2)]
    z = [back(g, 0, y_own, y_other[g], tile, tiles[g], F32) for g in range(2)]
    ended = []
    for c, dtype in enumerate((BF16, F32)):
        own, *out = pack([z[g][c] for g in range(2)], r2[c])
        ended.append(fold(own, [permute(out[e - 1], v_perm(e)) for e in ((3, 1, 2), (2, 1, 3))[c]], dtype))
    factor = (counts.shape[0] * lax.axis_size("rows")) ** (-0.5)
    z_proj = last(ended[1], permute(ended[0], ZH_PERM), factor)
    return (jnp.transpose(y_own), z_proj[None])


def solution(mesh):
    in_specs = (P("rows", "cols"), P("rows"), P("cols"), P("cols"), P("cols", None))
    out_specs = (P("rows", None), P("cols", "rows", None))
    return jax.shard_map(local, mesh=mesh, in_specs=in_specs, out_specs=out_specs, check_vma=False)
```

```python
import functools

import jax
import jax.numpy as jnp
from jax import lax
from jax.experimental import pallas as pl
from jax.experimental.pallas import tpu as pltpu
from jax.sharding import PartitionSpec as P

AXES = ("rows", "cols")
W = 256
STEP = 8
F32, BF16 = jnp.float32, jnp.bfloat16

NEAR, FAR = (3, 1), (1, 3)


def xor_perm(mask):
    pairs = []
    for d in range(128):
        r, zl, core = d >> 2, (d >> 1) & 1, d & 1
        dr, dzl, dcore = mask(core)
        pairs.append((d, ((r ^ dr) << 2) | ((zl ^ dzl) << 1) | (core ^ dcore)))
    return pairs


def u_perm(d):
    return xor_perm(lambda core: (d * (2 if core else 8), 0, 0))


def v_perm(d):
    return xor_perm(lambda core: (d * (8 if core else 2), 0, 0))


ZH_PERM = xor_perm(lambda core: (1, 0, 0))
ZL_PERM = xor_perm(lambda core: (0, 1, 0))
CORE_PERM = xor_perm(lambda core: (0, 0, 1))


def permute(a, perm):
    return lax.ppermute(a, AXES, perm)


def place():
    core = lax.rem(lax.axis_index("cols"), 2)
    return lax.axis_index("rows"), core


def block_of(r, core, g, d, e, k):
    return (r ^ (d * (8 - 6 * core) + e * (2 + 6 * core) + k)) * 2 + g


def slots(g, part):
    return [((NEAR[g] if part else 0) ^ (FAR[g] * i), e, k) for i in range(2) for k in (1, 0) for e in range(4)]


def params(mib):
    return pltpu.CompilerParams(vmem_limit_bytes=mib << 20)


def spec(space):
    return pl.BlockSpec(memory_space=space)


def context_kernel(all_ref, power_ref, shrink_ref, total_ref, inv_ref, tail_ref):
    power = jnp.exp(0.75 * jnp.log(all_ref[0:128, :].astype(F32)))
    power_ref[...] = 1.0 / power
    shrink_ref[...] = all_ref[128:256, :].astype(F32) * 0.25
    total_ref[...] = jnp.full((8, 128), jnp.sum(power), F32)
    wide = jnp.concatenate([all_ref[256:257, :], all_ref[257:258, :]], axis=1)
    inv_ref[...] = 1.0 / jnp.transpose(jnp.broadcast_to(wide.astype(F32), (128, W)))
    at = lax.broadcasted_iota(jnp.int32, (16, W), 0)
    low, mid, high = wide & 63, (wide >> 6) & 63, wide >> 12
    tail_ref[...] = jnp.where(at == 0, low, jnp.where(at == 1, mid, high)).astype(F32).astype(BF16)


def context(ctx_marg, discount, row_marg):
    square = jax.ShapeDtypeStruct((128, 128), F32)
    return pl.pallas_call(
        context_kernel,
        in_specs=[spec(pltpu.VMEM)],
        out_specs=[spec(pltpu.VMEM)] * 5,
        out_shape=(square, square, jax.ShapeDtypeStruct((8, 128), F32), jax.ShapeDtypeStruct((W, 128), F32),
                   jax.ShapeDtypeStruct((16, W), BF16)),
        compiler_params=params(2),
        cost_estimate=pl.CostEstimate(flops=1 << 18, bytes_accessed=1 << 18, transcendentals=1 << 15),
    )(jnp.concatenate([ctx_marg, discount, row_marg]).reshape(258, 128))


def fetch_block(counts_ref, in_ref, sem, g, part, s, i=0):
    r, core = place()
    d, e, k = slots(g, part)[s]
    at = pl.multiple_of(block_of(r, core, g, d ^ (FAR[g] * i), e, k) * W, W)
    return pltpu.make_async_copy(counts_ref.at[:, pl.ds(at, W)], in_ref.at[s + 8 * i], sem.at[s + 8 * i])


def prepare_kernel(part, *refs):
    if part == 1:
        tail_ref, counts_ref, *outs, in_a, in_b, sem_a, sem_b = refs
        bufs = ((in_a, sem_a), (in_b, sem_b))
    else:
        counts_ref, *outs, in_a, sem_a = refs
        bufs = ((in_a, sem_a),)
    copies = [(g, s) for g in range(len(outs)) for s in range(16)]
    for g, s in copies:
        fetch_block(counts_ref, *bufs[g], g, part, s).start()
    if part == 1:
        for out_ref in outs:
            out_ref[16 * W:16 * W + 16, :] = tail_ref[...]
    for g, s in copies:
        fetch_block(counts_ref, *bufs[g], g, part, s).wait()
        outs[g][s * W:(s + 1) * W, :] = bufs[g][0][s].astype(F32).astype(BF16)


def prepare(part, counts, *tail):
    rows = counts.shape[0]
    n = 1 + part
    return pl.pallas_call(
        functools.partial(prepare_kernel, part),
        in_specs=[spec(pltpu.VMEM)] * part + [spec(pl.ANY)],
        out_specs=[spec(pltpu.VMEM)] * n,
        out_shape=[jax.ShapeDtypeStruct((16 * W + 16 * part, W), BF16)] * n,
        scratch_shapes=[pltpu.VMEM((16, rows, W), jnp.int32)] * n + [pltpu.SemaphoreType.DMA((16,))] * n,
        compiler_params=params(38),
        cost_estimate=pl.CostEstimate(flops=1 << 22, bytes_accessed=n * (6 << 20), transcendentals=0),
    )(*tail, counts)


def tile_rows(counts, shrink, scale, inv_row):
    inv_row = jnp.concatenate([inv_row, inv_row], axis=1)
    excess = counts.astype(F32) - shrink
    return jnp.log(jnp.maximum(excess * scale * inv_row, 1.0)).astype(BF16)


def column_terms(ref, block):
    return jnp.concatenate([ref[pl.ds(2 * block, 1), :], ref[pl.ds(2 * block + 1, 1), :]], axis=1)


def whole_total(a_ref, b_ref):
    both = a_ref[0:1, :] + b_ref[0:1, :]
    return jnp.concatenate([both, both], axis=1)


def forward_kernel(total_ref, other_ref, inv_ref, power_ref, shrink_ref, sent_a, sent_b, kept_a, probes_ref, counts_ref,
                   tile_ref, y_ref, acc_ref, work_ref, in_ref, sem):
    r, core = place()
    total = whole_total(total_ref, other_ref)
    rows = inv_ref.shape[0]
    for s in range(16):
        fetch_block(counts_ref, in_ref, sem, 1, 0, s).start()
    acc_ref[...] = jnp.zeros_like(acc_ref)
    for part, g, blocks in ((1, 0, sent_a), (1, 1, sent_b), (0, 0, kept_a), (0, 1, None)):
        @pl.loop(0, 2)
        def _(i):
            sums = None
            if blocks is None:
                for n in range(8):
                    fetch_block(counts_ref, in_ref, sem, g, part, n, i).wait()
            for n, (d, e, k) in enumerate(slots(g, part)[:8]):
                block = block_of(r, core, g, d ^ (FAR[g] * i), e, k)
                at = pl.multiple_of(block * W, W)
                shrink = column_terms(shrink_ref, block)
                scale = column_terms(power_ref, block) * total
                if blocks is None:
                    source = in_ref.at[8 * i + n]
                else:
                    source = blocks.at[pl.ds(pl.multiple_of((8 * i + n) * rows, rows), rows)]
                out = work_ref.at[n] if part else tile_ref.at[16 * g + 8 * i + n]
                for q in range(0, rows, 32):
                    out[q:q + 32, :] = tile_rows(source[q:q + 32, :], shrink, scale, inv_ref[q:q + 32, :])
                term = jnp.dot(out[...], probes_ref[pl.ds(at, W), :], preferred_element_type=F32)
                sums = term if sums is None else sums + term
            acc_ref[...] += sums
    y_ref[...] = jnp.transpose(acc_ref[...])


def forward(total, other, inv_row, power, shrink, sent, kept, probes, counts):
    rows, width = inv_row.shape[0], probes.shape[1]
    vmem = spec(pltpu.VMEM)
    return pl.pallas_call(
        forward_kernel,
        in_specs=[vmem] * 9 + [spec(pl.ANY)],
        out_specs=[vmem, vmem],
        scratch_shapes=[
            pltpu.VMEM((rows, width), F32),
            pltpu.VMEM((STEP, rows, W), BF16),
            pltpu.VMEM((16, rows, W), jnp.int32),
            pltpu.SemaphoreType.DMA((16,)),
        ],
        out_shape=(jax.ShapeDtypeStruct((32, rows, W), BF16), jax.ShapeDtypeStruct((width, rows), F32)),
        compiler_params=params(30),
        cost_estimate=pl.CostEstimate(flops=1 << 31, bytes_accessed=28 << 20, transcendentals=1 << 22),
    )(total, other, inv_row, power, shrink, *sent, kept, probes, counts)


def other_kernel(group, half, total_ref, other_ref, power_ref, shrink_ref, count_ref, tile_ref, inv_ref):
    r, core = place()
    total = whole_total(total_ref, other_ref)
    rows = tile_ref.shape[1]
    tail = count_ref[16 * W:16 * W + 16, :].astype(F32)
    marg = tail[0:1, :] + tail[1:2, :] * 64.0 + tail[2:3, :] * 4096.0
    inv_ref[...] = 1.0 / jnp.transpose(jnp.broadcast_to(marg, (128, rows)))

    for n, (d, e, k) in enumerate(slots(group, 0)[8 * half:8 * half + 8]):
        block = block_of(r, core, group, d, e, k)
        shrink = column_terms(shrink_ref, block)
        scale = column_terms(power_ref, block) * total
        base = (8 * half + n) * rows
        for q in range(0, rows, 32):
            tile_ref[n, q:q + 32, :] = tile_rows(count_ref[base + q:base + q + 32, :], shrink, scale, inv_ref[q:q + 32, :])


def other_tile(group, half, total, other, power, shrink, received):
    vmem = spec(pltpu.VMEM)
    return pl.pallas_call(
        functools.partial(other_kernel, group, half),
        in_specs=[vmem] * 5,
        out_specs=vmem,
        scratch_shapes=[pltpu.VMEM((W, 128), F32)],
        out_shape=jax.ShapeDtypeStruct((8, W, W), BF16),
        compiler_params=params(4),
        cost_estimate=pl.CostEstimate(flops=1 << 24, bytes_accessed=4 << 20, transcendentals=1 << 20),
    )(total, other, power, shrink, received)


def back_kernel(base, half, y_own_ref, y_other_ref, own_ref, other_ref, *outs):
    for n in range(8):
        out = jnp.dot(y_own_ref[...], own_ref[base + half * 8 + n], preferred_element_type=F32)
        out = out + jnp.dot(y_other_ref[...], other_ref[n], preferred_element_type=F32)
        outs[n // 4][n % 4] = out.astype(outs[0].dtype)


def back(group, half, y_own, y_other, own, other, dtype):
    vmem = spec(pltpu.VMEM)
    return pl.pallas_call(
        functools.partial(back_kernel, group * 16, half),
        in_specs=[vmem] * 4,
        out_specs=[vmem] * 2,
        out_shape=[jax.ShapeDtypeStruct((4, y_own.shape[0], W), dtype)] * 2,
        compiler_params=params(4),
        cost_estimate=pl.CostEstimate(flops=1 << 29, bytes_accessed=4 << 20, transcendentals=0),
    )(y_own, y_other, own, other)


def pack_kernel(z_a, r_a, z_b, r_b, own_ref, *outs):
    for g, (z_ref, r_ref) in enumerate(((z_a, r_a), (z_b, r_b))):
        for e in range(4):
            total = z_ref[e] + r_ref[e].astype(F32)
            if e == 0:
                own_ref[g] = total
            else:
                outs[e - 1][g] = total.astype(BF16)


def pack(z, r):
    vmem = spec(pltpu.VMEM)
    width = z[0].shape[1]
    return pl.pallas_call(
        pack_kernel,
        in_specs=[vmem] * 4,
        out_specs=[vmem] * 4,
        out_shape=[jax.ShapeDtypeStruct((2, width, W), F32)] + [jax.ShapeDtypeStruct((2, width, W), BF16)] * 3,
        compiler_params=params(4),
        cost_estimate=pl.CostEstimate(flops=1 << 21, bytes_accessed=4 << 20, transcendentals=0),
    )(z[0], r[0], z[1], r[1])


def fold_kernel(own_ref, a_ref, b_ref, c_ref, out_ref):
    for g in range(2):
        total = own_ref[g] + a_ref[g].astype(F32) + b_ref[g].astype(F32) + c_ref[g].astype(F32)
        out_ref[g] = (jnp.transpose(total) if out_ref.dtype == F32 else total).astype(out_ref.dtype)


def fold(own, got, dtype):
    vmem = spec(pltpu.VMEM)
    return pl.pallas_call(
        fold_kernel,
        in_specs=[vmem] * 4,
        out_specs=vmem,
        out_shape=jax.ShapeDtypeStruct(own.shape, dtype),
        compiler_params=params(4),
        cost_estimate=pl.CostEstimate(flops=1 << 20, bytes_accessed=2 << 20, transcendentals=0),
    )(own, *got)


def last_kernel(factor, own_ref, got_ref, z_ref):
    for g in range(2):
        z_ref[g * W:(g + 1) * W, :] = (own_ref[g] + jnp.transpose(got_ref[g].astype(F32))) * factor


def last(own, got, factor):
    width = own.shape[1]
    vmem = spec(pltpu.VMEM)
    return pl.pallas_call(
        functools.partial(last_kernel, factor),
        in_specs=[vmem] * 2,
        out_specs=vmem,
        out_shape=jax.ShapeDtypeStruct((2 * W, width), F32),
        compiler_params=params(4),
        cost_estimate=pl.CostEstimate(flops=1 << 20, bytes_accessed=2 << 20, transcendentals=0),
    )(own, got)


def local(counts, row_marg, ctx_marg, discount, probes):
    power, shrink, total, inv_row, tail = context(ctx_marg, discount, row_marg)
    sent = prepare(1, counts, tail)
    total = total + permute(total, CORE_PERM)
    sent, total = lax.optimization_barrier((sent, total))
    received = [permute(sent[g], u_perm(NEAR[g])) for g in range(2)]
    other = permute(total, ZL_PERM)
    kept, = prepare(0, counts)
    tile, y_part = forward(total, other, inv_row, power, shrink, sent, kept, probes, counts)
    y_chip = (y_part + permute(y_part, CORE_PERM)).astype(BF16)
    y_own = (y_chip.astype(F32) + permute(y_chip, ZL_PERM).astype(F32)).astype(BF16)
    y_other = [permute(y_own, u_perm(NEAR[g])) for g in range(2)]

    tiles = [other_tile(g, 1, total, other, power, shrink, received[g]) for g in range(2)]
    y_other, tiles = zip(*[lax.optimization_barrier((y_other[g], tiles[g])) for g in range(2)])
    sends = [back(g, 1, y_own, y_other[g], tile, tiles[g], BF16) for g in range(2)]
    r2 = [[permute(sends[g][c], u_perm(FAR[g])) for g in range(2)] for c in range(2)]
    later = [other_tile(g, 0, total, other, power, shrink, received[g]) for g in range(2)]
    z = [back(g, 0, y_own, y_other[g], tile, later[g], F32) for g in range(2)]
    ended = []
    for c, dtype in enumerate((BF16, F32)):
        own, *out = pack([z[g][c] for g in range(2)], r2[c])
        ended.append(fold(own, [permute(out[e - 1], v_perm(e)) for e in ((3, 1, 2), (2, 1, 3))[c]], dtype))
    factor = (counts.shape[0] * lax.axis_size("rows")) ** (-0.5)
    z_proj = last(ended[1], permute(ended[0], ZH_PERM), factor)
    return (jnp.transpose(y_own), z_proj[None])


def solution(mesh):
    in_specs = (P("rows", "cols"), P("rows"), P("cols"), P("cols"), P("cols", None))
    out_specs = (P("rows", None), P("cols", "rows", None))
    return jax.shard_map(local, mesh=mesh, in_specs=in_specs, out_specs=out_specs, check_vma=False)
```
